32 devices in a mesh: rack: 8 (over z, core), cls: 4 (over y, x).
Axes of the slice: x: 2, y: 2, z: 4, core: 2. Of those that a mesh axis runs over, the one named last changes fastest.
Arguments:
- history: bfloat16 [4, 5120, 5120], P(None, 'rack', 'cls'), may hold values from -6 to 6
- rack_lag_coefficients: float32 [4, 5120], P(None, 'rack'), may hold values from -4 to 4
- class_lag_coefficients: float32 [4, 5120], P(None, 'cls'), may hold values from -4 to 4
- rack_reconcile_matrix: float32 [5120, 5120], P('rack', 'cls'), may hold values from -1 to 1
- class_reconcile_matrix: float32 [5120, 5120], P('rack', 'cls'), may hold values from -1 to 1
Outputs:
- reconciled: float32 [5120, 5120], P('rack', 'cls')
The draws below stay inside these ranges and needn't reach their ends.
All inputs are finite; a program needn't handle non-finite values.
Results may differ from the reference program's by a relative error of at most 0.0003.
Values sent between devices are 32-bit elements; how exact they have to be, the bound alone decides.
A program may use at most 128 MiB of HBM per device.

```python
import math
import jax
import jax.numpy as jnp
from jax import lax

NR = 5120
NC = 5120
LAGS = 4


def projection_like(key, order):
    key_off, key_diag = jax.random.split(key)
    row_ids = lax.broadcasted_iota(jnp.int32, (order, order), 0)
    col_ids = lax.broadcasted_iota(jnp.int32, (order, order), 1)
    offdiag = jax.random.normal(key_off, (order, order), jnp.float32) * (0.6 / math.sqrt(order))
    offdiag = jnp.clip(offdiag, -0.9, 0.9)
    diag_vals = jax.random.uniform(key_diag, (order, order), jnp.float32, 0.5, 1.0)
    return jnp.where(row_ids == col_ids, diag_vals, offdiag)


def draw_rack_reconcile_matrix(key, part):
    return projection_like(jax.random.fold_in(key, 11), NR)


def draw_class_reconcile_matrix(key, part):
    return projection_like(jax.random.fold_in(key, 23), NC)


def steps_of(rng, dims, cuts, low, top_value):
    def one(dim, shards_of):
        heights = jax.random.uniform(jax.random.fold_in(jax.random.fold_in(rng, 6), dim), (shards_of,), jnp.float32, low / len(cuts), top_value / len(cuts))
        return jnp.repeat(jnp.exp(heights), dims[dim] // shards_of).reshape((-1,) + (1,) * (len(dims) - dim - 1))

    gain = one(*cuts[0])
    for cut in cuts[1:]:
        gain = gain * one(*cut)
    return gain


def normal_values(own_key, extent, width, bound, cuts=(), dtype=jnp.bfloat16):
    values = width * jax.random.normal(own_key, extent, jnp.float32)
    if cuts:
        values = values * steps_of(own_key, extent, cuts, -0.22, 0.18)
    return jnp.clip(values, -bound, bound).astype(dtype)


def setup_inputs(seed: int = 0) -> dict:
    streams_of = jax.random.split(jax.random.key(seed), 6)
    return {
        "history": normal_values(streams_of[0], (LAGS, NR, NC), 1.0, 6.0, ((1, 8), (2, 4))),
        "rack_lag_coefficients": normal_values(streams_of[1], (LAGS, NR), 0.6, 4.0, ((1, 8),), jnp.float32),
        "class_lag_coefficients": normal_values(streams_of[2], (LAGS, NC), 0.6, 4.0, ((1, 4),), jnp.float32),
        "rack_reconcile_matrix": draw_rack_reconcile_matrix(jax.random.fold_in(streams_of[5], 71), 0),
        "class_reconcile_matrix": draw_class_reconcile_matrix(jax.random.fold_in(streams_of[5], 71), 0),
    }


def reference(history, rack_lag_coefficients, class_lag_coefficients, rack_reconcile_matrix, class_reconcile_matrix):
    predict_step = jnp.sum(history.astype(jnp.float32) * rack_lag_coefficients[:, :, None] * class_lag_coefficients[:, None, :], axis=0)
    lefthand_operand = jnp.dot(rack_reconcile_matrix, predict_step, precision=lax.Precision.HIGHEST, preferred_element_type=jnp.float32)
    return lax.dot_general(lefthand_operand, class_reconcile_matrix, (((1,), (1,)), ((), ())), precision=lax.Precision.HIGHEST, preferred_element_type=jnp.float32)
```

```python
import jax
import jax.numpy as jnp
from jax import lax
from jax.sharding import PartitionSpec as P


def split(x):
    high = lax.reduce_precision(x, 8, 7)
    return high.astype(jnp.bfloat16), (x - high).astype(jnp.bfloat16)


def dot3(a, b, dims):
    (a_hi, a_lo), (b_hi, b_lo) = a, b

    def one(p, q):
        return lax.dot_general(p, q, (dims, ((), ())), preferred_element_type=jnp.float32)

    return one(a_hi, b_hi) + (one(a_hi, b_lo) + one(a_lo, b_hi))


def swap(x, axis, size, distance):
    return lax.ppermute(x, axis, [(i, i ^ distance) for i in range(size)])


def gather_class_columns(block, size):
    if size & (size - 1):
        return lax.all_gather(block, "cls", axis=1, tiled=True)
    me = lax.axis_index("cls")
    rows, width = block.shape
    panel = jnp.zeros((rows, size * width), block.dtype)
    for distance in range(size):
        other = swap(block, "cls", size, distance) if distance else block
        panel = lax.dynamic_update_slice(panel, other, (0, (me ^ distance) * width))
    return panel


def scatter_class_columns(partial_terms, size):
    if size & (size - 1):
        return lax.psum_scatter(partial_terms, "cls", scatter_dimension=1, tiled=True)
    me = lax.axis_index("cls")
    rows, width = partial_terms.shape[0], partial_terms.shape[1] // size

    def owned_by(other):
        return lax.dynamic_slice(partial_terms, (0, other * width), (rows, width))

    total = owned_by(me)
    for distance in range(1, size):
        total = total + swap(owned_by(me ^ distance), "cls", size, distance)
    return total


def cuts_of(rows):
    if rows % 128:
        return [rows // 2, rows - rows // 2]
    tiles = rows // 128
    if tiles < 3:
        return [128] * tiles
    first = (tiles - 1) // 2
    return [128 * (tiles - 1 - first), 128 * first, 128]


def make_body(n_rack, n_cls):
    def body(
        history,
        rack_lag_coefficients,
        class_lag_coefficients,
        rack_reconcile_matrix,
        class_reconcile_matrix,
    ):
        predict_step = jnp.sum(
            history.astype(jnp.float32)
            * rack_lag_coefficients[:, :, None]
            * class_lag_coefficients[:, None, :],
            axis=0,
        )
        forecast = lax.all_gather(predict_step, "rack", axis=0, tiled=True)
        panel = gather_class_columns(rack_reconcile_matrix, n_cls)
        left = split(dot3(split(panel), split(forecast), ((1,), (0,))))

        rows = class_reconcile_matrix.shape[0]
        blocks = n_rack // n_cls
        parts, start = [], 0
        for height in cuts_of(rows):
            part = lax.slice_in_dim(class_reconcile_matrix, start, start + height, axis=0)
            if start + height == rows:
                part, _ = lax.optimization_barrier((part, panel))
            gathered = lax.all_gather(part, "rack", axis=0, tiled=True)
            terms = dot3(left, split(gathered), ((1,), (1,)))
            owned = scatter_class_columns(terms, n_cls)
            parts.append(jnp.split(owned, blocks, axis=1))
            start += height
        return jnp.concatenate([part[b] for b in range(blocks) for part in parts], axis=1)

    return body


def solution(mesh):
    placed = (
        P(None, "rack", "cls"),
        P(None, "rack"),
        P(None, "cls"),
        P("rack", "cls"),
        P("rack", "cls"),
    )
    return jax.shard_map(
        make_body(mesh.shape["rack"], mesh.shape["cls"]),
        mesh=mesh,
        in_specs=placed,
        out_specs=P("rack", "cls"),
        check_vma=False,
    )
```

```python
import jax
import jax.numpy as jnp
from jax import lax
from jax.sharding import PartitionSpec as P


def split(x):
    high = lax.reduce_precision(x, 8, 7)
    return high.astype(jnp.bfloat16), (x - high).astype(jnp.bfloat16)


def dot3(a, b, dims):
    (a_hi, a_lo), (b_hi, b_lo) = a, b

    def one(p, q):
        return lax.dot_general(p, q, (dims, ((), ())), preferred_element_type=jnp.float32)

    return one(a_hi, b_hi) + (one(a_hi, b_lo) + one(a_lo, b_hi))


def swap(x, axis, size, distance):
    return lax.ppermute(x, axis, [(i, i ^ distance) for i in range(size)])


def after(x, other):
    corner = lax.slice(other, (0, 0), (8, min(128, other.shape[1])))
    return lax.optimization_barrier((x, corner))[0]


def to_plane(block, n_rack, n_cls):
    moves = [
        ((2 * p + q) * n_cls + c, (2 * c + q) * n_cls + p)
        for p in range(n_cls)
        for q in range(2)
        for c in range(n_cls)
    ]
    return lax.ppermute(block, ("rack", "cls"), moves)


def node_columns(block, n_rack, n_cls, behind):
    core = lax.rem(lax.axis_index("rack"), 2)
    rows, width = block.shape[0], block.shape[1] // 2
    mine = lax.dynamic_slice(block, (0, core * width), (rows, width))
    other = lax.dynamic_slice(block, (0, (1 - core) * width), (rows, width))
    other = swap(other, "rack", n_rack, 1)
    pair = jnp.where(core == 0, jnp.stack([mine, other]), jnp.stack([other, mine]))
    pair = after(pair.reshape(2 * rows, width), behind)
    if n_cls & (n_cls - 1):
        return lax.all_gather(pair, "cls", axis=0, tiled=True)
    me = lax.axis_index("cls")
    strip = jnp.zeros((n_cls * 2 * rows, width), block.dtype)
    for distance in range(n_cls):
        part = swap(pair, "cls", n_cls, distance) if distance else pair
        strip = lax.dynamic_update_slice(strip, part, ((me ^ distance) * 2 * rows, 0))
    return strip


def scatter_rack_rows(terms, n_rack):
    planes = n_rack // 2
    plane, core = lax.div(lax.axis_index("rack"), 2), lax.rem(lax.axis_index("rack"), 2)
    rows, width = terms.shape[0] // n_rack, terms.shape[1]
    terms = terms.reshape(planes, 2, rows, width)

    def of_core(q):
        return lax.dynamic_slice(terms, (0, q, 0, 0), (planes, 1, rows, width))[:, 0]

    sums = of_core(core) + swap(of_core(1 - core), "rack", n_rack, 1)

    def bound_for(target):
        target = jnp.clip(target, 0, planes - 1)
        return lax.dynamic_slice(sums, (target, 0, 0), (1, rows, width))[0]

    total = bound_for(plane)
    up = down = None
    for turn in range(1, planes):
        rising, falling = bound_for(plane + planes - turn), bound_for(plane - planes + turn)
        if up is not None:
            rising, falling = rising + up, falling + down
        up = lax.ppermute(
            rising, "rack", [(2 * p + q, 2 * p + 2 + q) for p in range(turn) for q in range(2)]
        )
        down = lax.ppermute(
            falling,
            "rack",
            [(2 * p + q, 2 * p - 2 + q) for p in range(planes - turn, planes) for q in range(2)],
        )
    return total + up + down


def scatter_class_columns(partial_terms, size):
    if size & (size - 1):
        return lax.psum_scatter(partial_terms, "cls", scatter_dimension=1, tiled=True)
    me = lax.axis_index("cls")
    rows, width = partial_terms.shape[0], partial_terms.shape[1] // size

    def owned_by(other):
        return lax.dynamic_slice(partial_terms, (0, other * width), (rows, width))

    total = owned_by(me)
    for distance in range(1, size):
        total = total + swap(owned_by(me ^ distance), "cls", size, distance)
    return total


def cuts_of(rows):
    if rows % 128:
        return [rows // 2, rows - rows // 2]
    tiles = rows // 128
    if tiles < 4:
        return [128] * tiles
    return [128, 128 * ((tiles - 2) // 2), 128 * (tiles - 2 - (tiles - 2) // 2), 128]


def make_body(n_rack, n_cls):
    def body(
        history,
        rack_lag_coefficients,
        class_lag_coefficients,
        rack_reconcile_matrix,
        class_reconcile_matrix,
    ):
        predict_step = jnp.sum(
            history.astype(jnp.float32)
            * rack_lag_coefficients[:, :, None]
            * class_lag_coefficients[:, None, :],
            axis=0,
        )
        forecast = split(predict_step)
        rows = class_reconcile_matrix.shape[0]
        blocks = n_rack // n_cls
        moved = to_plane(rack_reconcile_matrix, n_rack, n_cls)
        gathered, start = [], 0
        for height in cuts_of(rows):
            part = lax.slice_in_dim(class_reconcile_matrix, start, start + height, axis=0)
            if len(gathered) > 1:
                part = after(part, gathered[-2] if len(gathered) > 2 else moved)
            gathered.append(lax.all_gather(part, "rack", axis=0, tiled=True))
            start += height
        strip = split(node_columns(moved, n_rack, n_cls, gathered[0]))
        parts = []
        for chunk in gathered:
            terms = dot3(forecast, split(chunk), ((1,), (1,)))
            owned = scatter_class_columns(terms, n_cls)
            sums = dot3(strip, split(owned), ((1,), (0,)))
            owned = scatter_rack_rows(sums, n_rack)
            parts.append(jnp.split(owned, blocks, axis=1))
        return jnp.concatenate([part[b] for b in range(blocks) for part in parts], axis=1)

    return body


def solution(mesh):
    placed = (
        P(None, "rack", "cls"),
        P(None, "rack"),
        P(None, "cls"),
        P("rack", "cls"),
        P("rack", "cls"),
    )
    return jax.shard_map(
        make_body(mesh.shape["rack"], mesh.shape["cls"]),
        mesh=mesh,
        in_specs=placed,
        out_specs=P("rack", "cls"),
        check_vma=False,
    )
```

```python
import jax
import jax.numpy as jnp
from jax import lax
from jax.sharding import PartitionSpec as P


def split(x):
    high = lax.reduce_precision(x, 8, 7)
    return high.astype(jnp.bfloat16), (x - high).astype(jnp.bfloat16)


def dot3(a, b, dims):
    (a_hi, a_lo), (b_hi, b_lo) = a, b

    def one(p, q):
        return lax.dot_general(p, q, (dims, ((), ())), preferred_element_type=jnp.float32)

    return one(a_hi, b_hi) + (one(a_hi, b_lo) + one(a_lo, b_hi))


def swap(x, axis, size, distance):
    return lax.ppermute(x, axis, [(i, i ^ distance) for i in range(size)])


def gather_class_columns(block, size):
    if size & (size - 1):
        return lax.all_gather(block, "cls", axis=1, tiled=True)
    me = lax.axis_index("cls")
    rows, width = block.shape
    panel = jnp.zeros((rows, size * width), block.dtype)
    for distance in range(size):
        other = swap(block, "cls", size, distance) if distance else block
        panel = lax.dynamic_update_slice(panel, other, (0, (me ^ distance) * width))
    return panel


def scatter_class_columns(partial_terms, size):
    if size & (size - 1):
        return lax.psum_scatter(partial_terms, "cls", scatter_dimension=1, tiled=True)
    me = lax.axis_index("cls")
    rows, width = partial_terms.shape[0], partial_terms.shape[1] // size

    def owned_by(other):
        return lax.dynamic_slice(partial_terms, (0, other * width), (rows, width))

    total = owned_by(me)
    for distance in range(1, size):
        total = total + swap(owned_by(me ^ distance), "cls", size, distance)
    return total


def cuts_of(rows):
    if rows % 128:
        return [rows // 2, rows - rows // 2]
    tiles = rows // 128
    if tiles < 3:
        return [128] * tiles
    return [128 * (tiles // 2)] + [128] * (tiles - tiles // 2)


def make_body(n_rack, n_cls):
    def body(
        history,
        rack_lag_coefficients,
        class_lag_coefficients,
        rack_reconcile_matrix,
        class_reconcile_matrix,
    ):
        predict_step = jnp.sum(
            history.astype(jnp.float32)
            * rack_lag_coefficients[:, :, None]
            * class_lag_coefficients[:, None, :],
            axis=0,
        )
        forecast = lax.all_gather(predict_step, "rack", axis=0, tiled=True)
        panel = gather_class_columns(rack_reconcile_matrix, n_cls)
        product = dot3(split(panel), split(forecast), ((1,), (0,)))
        left = split(product)

        rows = class_reconcile_matrix.shape[0]
        blocks = n_rack // n_cls
        parts, start = [], 0
        for height in cuts_of(rows):
            part = lax.slice_in_dim(class_reconcile_matrix, start, start + height, axis=0)
            if start:
                part = part + 0.0 * product[:1, :1]
            gathered = lax.all_gather(part, "rack", axis=0, tiled=True)
            terms = dot3(left, split(gathered), ((1,), (1,)))
            owned = scatter_class_columns(terms, n_cls)
            parts.append(jnp.split(owned, blocks, axis=1))
            start += height
        return jnp.concatenate([part[b] for b in range(blocks) for part in parts], axis=1)

    return body


def solution(mesh):
    placed = (
        P(None, "rack", "cls"),
        P(None, "rack"),
        P(None, "cls"),
        P("rack", "cls"),
        P("rack", "cls"),
    )
    return jax.shard_map(
        make_body(mesh.shape["rack"], mesh.shape["cls"]),
        mesh=mesh,
        in_specs=placed,
        out_specs=P("rack", "cls"),
        check_vma=False,
    )
```
